32 devices in a mesh: grp: 2 (over x), exp: 16 (over z, y, core).
Axes of the slice: x: 2, y: 2, z: 4, core: 2. Of those that a mesh axis runs over, the one named last changes fastest.
Arguments:
- tokens: bfloat16 [4096, 4096], P(('grp', 'exp')), parts along dimension 0, may hold values from -6 to 6
- upstream: bfloat16 [4096, 4096], P(('grp', 'exp')), parts along dimension 0, may hold values from -6 to 6
- expert_ids: int32 [4096, 8], P(('grp', 'exp')), parts along dimension 0, may hold values from 0 to 127, as said below
- gate_values: float32 [4096, 8], P(('grp', 'exp')), parts along dimension 0, may hold values from 0.05 to 1
- w_gate: bfloat16 [16, 192, 4096], P('exp'), may hold values from -0.09375 to 0.09375
- w_up: bfloat16 [16, 192, 4096], P('exp'), may hold values from -0.09375 to 0.09375
- w_down: bfloat16 [16, 192, 4096], P('exp'), may hold values from -0.15625 to 0.15625
Outputs:
- d_tokens: bfloat16 [4096, 4096], P(('grp', 'exp')), parts along dimension 0
- grad_gate: bfloat16 [32, 192, 4096], P(('grp', 'exp')), parts along dimension 0
- grad_up: bfloat16 [32, 192, 4096], P(('grp', 'exp')), parts along dimension 0
- grad_down: bfloat16 [32, 192, 4096], P(('grp', 'exp')), parts along dimension 0
The draws below stay inside these ranges and needn't reach their ends.
There are 2 independent parts, one for each index of `grp`. The reference program is written for one: setup_inputs(seed, part) draws one part's arguments, and reference() takes and returns one part's arrays. A program takes and returns all parts, laid end to end along the dimension named above; an argument that names none is the same for every part. Nothing has to cross between parts.
Inputs may be any that keep to these rules, and one draw needn't show every extreme that they name: `expert_ids`: each token names 8 different experts, at most one of them below 2. Among one device's 128 tokens at most 16 name any one expert below 2, and some expert below 2 is named by exactly 16 tokens on every device.
All inputs are finite; a program needn't handle non-finite values.
Results may differ from the reference program's by a relative error of at most 0.0064.
Values may be sent and summed in bfloat16 or wider, within the bound.
No kernel may reach another device: no remote copies, remote signals or barrier semaphores. Data moves between devices by JAX's collectives and lax.ppermute only.
A program may use at most 128 MiB of HBM per device.

```python
import math
import jax
import jax.numpy as jnp
from jax import lax

D = 4096
F = 1536
EXPERTS = 128
TOPK = 8
TILES = 8
TOK_DEV = 128
FT = 192
CAP = 16
E_WIN = 2
TOKENS = 2048
N_EXP = 16


def draw_expert_ids(key, part):
    key = jax.random.fold_in(key, 11)
    blocks = TOKENS // TOK_DEV
    k_hot, k_top, k_count, k_perm, k_start, k_place = jax.random.split(key, 6)
    hottest = jax.random.randint(k_hot, (), 0, E_WIN)
    highest = jax.random.randint(k_top, (E_WIN,), CAP // 2, CAP + 1)
    counts = jax.random.randint(k_count, (blocks, E_WIN), 0, 1 << 20) % (highest[None, :] + 1)
    counts = jnp.where(jnp.arange(E_WIN)[None, :] == hottest, CAP, counts)
    bounds = jnp.cumsum(counts, axis=1)
    orders = jax.vmap(lambda k: jax.random.permutation(k, TOK_DEV))(jax.random.split(k_perm, blocks))
    window = jnp.sum((orders[:, :, None] >= bounds[:, None, :]).astype(jnp.int32), axis=2).reshape(TOKENS)
    start = jax.random.randint(k_start, (TOKENS,), 0, EXPERTS - E_WIN)
    place = jax.random.randint(k_place, (TOKENS,), 0, TOPK)
    column = jnp.arange(TOPK)[None, :]
    others = E_WIN + (start[:, None] + column) % (EXPERTS - E_WIN)
    chosen = jnp.where((column == place[:, None]) & (window[:, None] < E_WIN), window[:, None], others)
    return chosen.astype(jnp.int32)


def steps_of(own_key, dims, pieces, least, largest):
    def one(position, blocks):
        steps = jax.random.uniform(jax.random.fold_in(jax.random.fold_in(own_key, 6), position), (blocks,), jnp.float32, least / len(pieces), largest / len(pieces))
        return jnp.repeat(jnp.exp(steps), dims[position] // blocks).reshape((-1,) + (1,) * (len(dims) - position - 1))

    gain = one(*pieces[0])
    for cut in pieces[1:]:
        gain = gain * one(*cut)
    return gain


def bell_draw(own_key, extent, deviation, limit, cuts=(), kind=jnp.bfloat16):
    result = jax.random.normal(own_key, extent, jnp.float32) * deviation
    if len(cuts) > 0:
        result = steps_of(own_key, extent, cuts, -0.22, 0.18) * result
    return jnp.clip(result, min=-limit, max=limit).astype(kind)


def setup_inputs(seed: int = 0, part: int = 0) -> dict:
    streams_of = jax.random.split(jax.random.key(seed), 8)
    part_splits = jax.random.split(jax.random.fold_in(streams_of[7], part), 8)
    return {
        "tokens": bell_draw(part_splits[0], (TOKENS, D), 1.0, 6.0, ((0, 16),)),
        "upstream": bell_draw(part_splits[1], (TOKENS, D), 1.0, 6.0, ((0, 16),)),
        "expert_ids": draw_expert_ids(jax.random.fold_in(jax.random.fold_in(streams_of[7], part), 71), part),
        "gate_values": jnp.clip(jnp.exp(math.log(1.0) - 2.9957323 * jax.random.uniform(part_splits[3], (TOKENS, TOPK), jnp.float32) ** steps_of(part_splits[3], (TOKENS, TOPK), ((0, 16),), -0.2, 0.2)), 0.05, 1.0),
        "w_gate": bell_draw(streams_of[4], (E_WIN * TILES, FT, D), D ** -0.5, 0.09375, ((0, 16),)),
        "w_up": bell_draw(streams_of[5], (E_WIN * TILES, FT, D), D ** -0.5, 0.09375, ((0, 16),)),
        "w_down": bell_draw(streams_of[6], (E_WIN * TILES, FT, D), F ** -0.5, 0.15625, ((0, 16),)),
    }


def reference(tokens, upstream, expert_ids, gate_values, w_gate, w_up, w_down):
    rows = N_EXP * CAP
    inside = expert_ids < E_WIN
    chosen = jnp.sum(jnp.where(inside, expert_ids, 0), axis=1).astype(jnp.int32)
    has_slot = jnp.any(inside, axis=1)
    weight = jnp.sum(jnp.where(inside, gate_values, jnp.zeros_like(gate_values)), axis=1)
    scaled = (upstream.astype(jnp.float32) * weight[:, None]).astype(jnp.bfloat16)
    member = ((chosen[:, None] == jnp.arange(E_WIN, dtype=jnp.int32)[None, :]) & has_slot[:, None]).astype(jnp.int32)
    ranking = jnp.cumsum(member.reshape(N_EXP, TOK_DEV, E_WIN), axis=1).reshape(TOKENS, E_WIN) - 1
    rank = jnp.sum(member * ranking, axis=1).astype(jnp.int32)
    source = (jnp.arange(TOKENS, dtype=jnp.int32) // TOK_DEV).astype(jnp.int32)
    where_to = jnp.where(has_slot, chosen * rows + source * CAP + rank, E_WIN * rows).astype(jnp.int32)
    table = jnp.full((E_WIN * rows + 1,), TOKENS, dtype=jnp.int32).at[where_to].set(jnp.arange(TOKENS, dtype=jnp.int32))
    table = table[:E_WIN * rows].reshape(E_WIN, rows)
    padded_x = jnp.concatenate([tokens, jnp.zeros((1, D), tokens.dtype)], axis=0)
    padded_z = jnp.concatenate([scaled, jnp.zeros((1, D), scaled.dtype)], axis=0)

    def expert(args):
        index, wg, wu, wd = args
        row_x = padded_x[index]
        row_z = padded_z[index]
        wg_full = wg.reshape(F, D)
        wu_full = wu.reshape(F, D)
        wd_full = wd.reshape(F, D)
        pre_gate = jnp.dot(row_x, wg_full.T, preferred_element_type=jnp.float32)
        pre_up = jnp.dot(row_x, wu_full.T, preferred_element_type=jnp.float32)
        sigma = jax.nn.sigmoid(pre_gate)
        active = pre_gate * sigma
        hidden = (active * pre_up).astype(jnp.bfloat16)
        d_hidden = jnp.dot(row_z, wd_full.T, preferred_element_type=jnp.float32)
        d_gate = (d_hidden * pre_up * sigma * (1.0 + pre_gate * (1.0 - sigma))).astype(jnp.bfloat16)
        d_up = (d_hidden * active).astype(jnp.bfloat16)
        grad_g = jnp.dot(d_gate.T, row_x, preferred_element_type=jnp.float32).astype(jnp.bfloat16)
        grad_u = jnp.dot(d_up.T, row_x, preferred_element_type=jnp.float32).astype(jnp.bfloat16)
        grad_d = jnp.dot(hidden.T, row_z, preferred_element_type=jnp.float32).astype(jnp.bfloat16)
        tiled = jnp.einsum("rtf,tfd->rtd", d_gate.reshape(rows, TILES, FT).astype(jnp.float32), wg.astype(jnp.float32))
        tiled = tiled + jnp.einsum("rtf,tfd->rtd", d_up.reshape(rows, TILES, FT).astype(jnp.float32), wu.astype(jnp.float32))
        rounded = lax.optimization_barrier(tiled.astype(jnp.bfloat16))
        summed = jnp.sum(rounded.astype(jnp.float32), axis=1).astype(jnp.bfloat16)
        return summed, grad_g.reshape(TILES, FT, D), grad_u.reshape(TILES, FT, D), grad_d.reshape(TILES, FT, D)

    shaped = (table, w_gate.reshape(E_WIN, TILES, FT, D), w_up.reshape(E_WIN, TILES, FT, D), w_down.reshape(E_WIN, TILES, FT, D))
    summed, grad_g, grad_u, grad_d = lax.map(expert, shaped)
    d_tokens = jnp.zeros((TOKENS + 1, D), jnp.float32).at[table.reshape(-1)].add(summed.reshape(E_WIN * rows, D).astype(jnp.float32))
    d_tokens = d_tokens[:TOKENS].astype(jnp.bfloat16)
    return (d_tokens, grad_g.reshape(E_WIN * TILES, FT, D), grad_u.reshape(E_WIN * TILES, FT, D), grad_d.reshape(E_WIN * TILES, FT, D))
```

```python
import functools

import jax
import jax.numpy as jnp
from jax import lax
from jax.experimental import pallas as pl
from jax.experimental.pallas import tpu as pltpu
from jax.sharding import PartitionSpec as P

TILES = 8
CAP = 16
BF = jnp.bfloat16
F32 = jnp.float32
VMEM = pl.BlockSpec(memory_space=pltpu.VMEM)
SMEM = pl.BlockSpec(memory_space=pltpu.SMEM)
PARAMS = pltpu.CompilerParams(vmem_limit_bytes=48 * 1024 * 1024)


def dot(left, right, left_dim, right_dim):
    return lax.dot_general(
        left, right, (((left_dim,), (right_dim,)), ((), ())), preferred_element_type=F32
    )


def pack_kernel(window, own_ref, ids_ref, gate_ref, tokens_ref, upstream_ref, *out):
    select_ref, blocks = out[0], out[1:]
    count, width = tokens_ref.shape
    ids = ids_ref[...]
    inside = ids < window
    chosen = jnp.sum(jnp.where(inside, ids, 0).astype(F32), axis=1, keepdims=True).astype(jnp.int32)
    has_slot = jnp.sum(inside.astype(F32), axis=1, keepdims=True) > 0.0
    weight = jnp.sum(jnp.where(inside, gate_ref[...], 0.0), axis=1, keepdims=True)
    shift = chosen - own_ref[0]
    shift = jnp.where(shift < 0, shift + window, shift)
    lanes = window * CAP
    lane = lax.broadcasted_iota(jnp.int32, (count, lanes), 1)
    first = shift * CAP
    member = ((lane >= first) & (lane < first + CAP) & has_slot).astype(F32)
    row = lax.broadcasted_iota(jnp.int32, (count, count), 0)
    col = lax.broadcasted_iota(jnp.int32, (count, count), 1)
    before = (col < row).astype(BF)
    earlier = dot(before, member.astype(BF), 1, 0)
    position = lane - first
    select = ((member > 0.0) & (position.astype(F32) == earlier)).astype(BF)
    select_ref[...] = select
    step = min(1024, width)
    for at in range(0, width, step):
        cols = pl.ds(at, step)
        x = dot(select, tokens_ref[:, cols], 0, 0).astype(BF)
        scaled = (upstream_ref[:, cols].astype(F32) * weight).astype(BF)
        z = dot(select, scaled, 0, 0).astype(BF)
        for k in range(window):
            part = slice(k * CAP, (k + 1) * CAP)
            blocks[k][:CAP, cols] = x[part]
            blocks[k][CAP:, cols] = z[part]


def expert_kernel(count, *refs):
    blocks, refs = refs[:count], refs[count:]
    gate_ref, up_ref, down_ref, x_ref, z_ref, dg_ref, du_ref, hidden_ref = refs[:8]
    parts = refs[8:]
    for j, block in enumerate(blocks):
        x_ref[j * CAP : (j + 1) * CAP, :] = block[:CAP, :]
        z_ref[j * CAP : (j + 1) * CAP, :] = block[CAP:, :]
    x = x_ref[...]
    pre_gate = dot(x, gate_ref[...], 1, 1)
    pre_up = dot(x, up_ref[...], 1, 1)
    d_hidden = dot(z_ref[...], down_ref[...], 1, 1)
    sigma = 1.0 / (1.0 + jnp.exp(-pre_gate))
    active = pre_gate * sigma
    hidden_ref[...] = (active * pre_up).astype(BF)
    d_gate = (d_hidden * pre_up * sigma * (1.0 + pre_gate * (1.0 - sigma))).astype(BF)
    d_up = (d_hidden * active).astype(BF)
    dg_ref[...] = d_gate
    du_ref[...] = d_up
    half = count * CAP // 2
    width = gate_ref.shape[1]
    step = min(1024, width)
    for at in range(0, width, step):
        cols = pl.ds(at, step)
        value = dot(d_gate, gate_ref[:, cols], 1, 0) + dot(d_up, up_ref[:, cols], 1, 0)
        value = value.astype(BF)
        parts[0][:, cols] = value[:half]
        parts[1][:, cols] = value[half:]


def grad_kernel(count, *refs):
    out = refs[-1]
    total = None
    for j in range(count):
        term = dot(refs[j][...], refs[count + j][...], 0, 0)
        total = term if total is None else total + term
    out[...] = total.astype(BF)


def sum_kernel(terms, *refs):
    outs = refs[terms:]
    rows = outs[0].shape[0]
    for j, out in enumerate(outs):
        total = refs[0][j * rows : (j + 1) * rows, :].astype(F32)
        for ref in refs[1:terms]:
            total = total + ref[j * rows : (j + 1) * rows, :].astype(F32)
        out[...] = total.astype(BF)


def unpack_kernel(count, select_ref, *refs):
    out = refs[-1]
    width = out.shape[1]
    step = min(1024, width)
    for at in range(0, width, step):
        cols = pl.ds(at, step)
        rows = jnp.concatenate([refs[k][:, cols] for k in range(count)], axis=0)
        out[:, cols] = dot(select_ref[...], rows, 1, 0).astype(BF)


def call(kernel, out_shape, *args, smem=0):
    return pl.pallas_call(
        kernel,
        out_shape=out_shape,
        in_specs=[SMEM] * smem + [VMEM] * (len(args) - smem),
        out_specs=jax.tree.map(lambda _: VMEM, out_shape),
        compiler_params=PARAMS,
    )(*args)


def shape(*dims):
    return jax.ShapeDtypeStruct(dims, BF)


def grads(lefts, rights):
    count = len(lefts)
    hidden, width = lefts[0].shape[1], rights[0].shape[1]
    step = min(1024, width)
    return pl.pallas_call(
        functools.partial(grad_kernel, count),
        grid=(width // step,),
        out_shape=shape(hidden, width),
        in_specs=[pl.BlockSpec(a.shape, lambda i: (0, 0)) for a in lefts]
        + [pl.BlockSpec((a.shape[0], step), lambda i: (0, i)) for a in rights],
        out_specs=pl.BlockSpec((hidden, step), lambda i: (0, i)),
        compiler_params=PARAMS,
    )(*lefts, *rights)


def on_device(tokens, upstream, expert_ids, gate_values, w_gate, w_up, w_down):
    devices = lax.axis_size("exp")
    window = devices // TILES
    count, width = tokens.shape
    hidden = w_gate.shape[1]
    own = lax.axis_index("exp") // TILES

    def swap(a, bits):
        return lax.ppermute(a, "exp", [(i, i ^ bits) for i in range(devices)])

    def turn(a, k):
        return lax.ppermute(a, "exp", [(i, (i + k * TILES) % devices) for i in range(devices)])

    packed = call(
        functools.partial(pack_kernel, window),
        [shape(count, window * CAP)] + [shape(2 * CAP, width)] * window,
        own.astype(jnp.int32)[None],
        expert_ids,
        gate_values,
        tokens,
        upstream,
        smem=1,
    )
    select, packed = packed[0], packed[1:]
    blocks = [packed[0]] + [turn(packed[k], k) for k in range(1, window)]
    done = []
    for block in blocks:
        near = [block] + [swap(block, bits) for bits in (2, 4, 6)]
        both = near + [swap(b, 1) for b in near]
        rows = len(both) * CAP
        done.append(
            call(
                functools.partial(expert_kernel, len(both)),
                [shape(rows, width)] * 2 + [shape(rows, hidden)] * 3 + [shape(rows // 2, width)] * 2,
                *both,
                w_gate[0],
                w_up[0],
                w_down[0],
            )
        )
    returned = []
    for k, result in enumerate(done):
        mine, other = result[5:]
        pieces = call(functools.partial(sum_kernel, 2), [shape(CAP, width)] * 4, mine, swap(other, 1))
        pieces = [pieces[0]] + [swap(pieces[j], 2 * j) for j in (1, 2, 3)]
        whole = call(functools.partial(sum_kernel, 4), [shape(CAP, width)], *pieces)[0]
        returned.append(whole if k == 0 else turn(whole, window - k))
    grad_gate = grads([r[2] for r in done], [r[0] for r in done])
    grad_up = grads([r[3] for r in done], [r[0] for r in done])
    grad_down = grads([r[4] for r in done], [r[1] for r in done])
    d_tokens = call(
        functools.partial(unpack_kernel, window), shape(count, width), select, *returned
    )
    return (d_tokens, grad_gate[None], grad_up[None], grad_down[None])


def solution(mesh):
    rows = P(("grp", "exp"), None)
    tiles = P("exp", None, None)
    grown = P(("grp", "exp"), None, None)
    return jax.shard_map(
        on_device,
        mesh=mesh,
        in_specs=(rows, rows, rows, rows, tiles, tiles, tiles),
        out_specs=(rows, grown, grown, grown),
        check_vma=False,
    )
```

```python
import functools

import jax
import jax.numpy as jnp
from jax import lax
from jax.experimental import pallas as pl
from jax.experimental.pallas import tpu as pltpu
from jax.sharding import PartitionSpec as P

TILES = 8
CAP = 16
BF = jnp.bfloat16
F32 = jnp.float32
VMEM = pl.BlockSpec(memory_space=pltpu.VMEM)
SMEM = pl.BlockSpec(memory_space=pltpu.SMEM)
HBM = pl.BlockSpec(memory_space=pltpu.HBM)
STEP = 1024


def params(mib):
    return pltpu.CompilerParams(vmem_limit_bytes=mib * 1024 * 1024)


def dot(left, right, left_dim, right_dim):
    return lax.dot_general(
        left, right, (((left_dim,), (right_dim,)), ((), ())), preferred_element_type=F32
    )


def pack_kernel(window, own_ref, ids_hbm, gate_hbm, tokens_hbm, upstream_hbm, *refs):
    select_ref, blocks = refs[0], refs[1 : window + 1]
    ids_ref, gate_ref, tokens_ref, upstream_ref, small, large = refs[window + 1 :]
    count, width = tokens_ref.shape
    first_copies = [
        pltpu.make_async_copy(ids_hbm, ids_ref, small.at[0]),
        pltpu.make_async_copy(gate_hbm, gate_ref, small.at[1]),
    ]
    step = min(STEP, width)
    copies = []
    for j, at in enumerate(range(0, width, step)):
        cols = pl.ds(at, step)
        copies.append(
            (
                pltpu.make_async_copy(tokens_hbm.at[:, cols], tokens_ref.at[:, cols], large.at[2 * j]),
                pltpu.make_async_copy(
                    upstream_hbm.at[:, cols], upstream_ref.at[:, cols], large.at[2 * j + 1]
                ),
            )
        )
    for copy in first_copies:
        copy.start()
    for pair in copies:
        for copy in pair:
            copy.start()
    for copy in first_copies:
        copy.wait()
    ids = ids_ref[...]
    inside = ids < window
    chosen = jnp.sum(jnp.where(inside, ids, 0).astype(F32), axis=0, keepdims=True).astype(jnp.int32)
    has_slot = jnp.sum(inside.astype(F32), axis=0, keepdims=True) > 0.0
    weight = jnp.sum(jnp.where(inside, gate_ref[...], 0.0), axis=0, keepdims=True)
    shift = chosen - own_ref[0]
    shift = jnp.where(shift < 0, shift + window, shift)
    slots = window * CAP
    slot = lax.broadcasted_iota(jnp.int32, (slots, count), 0)
    first = shift * CAP
    member = ((slot >= first) & (slot < first + CAP) & has_slot).astype(F32)
    row = lax.broadcasted_iota(jnp.int32, (count, count), 0)
    col = lax.broadcasted_iota(jnp.int32, (count, count), 1)
    before = (row < col).astype(BF)
    earlier = dot(member.astype(BF), before, 1, 0)
    select = ((member > 0.0) & ((slot - first).astype(F32) == earlier)).astype(F32)
    scale = jnp.sum(select * weight, axis=1, keepdims=True)
    select = select.astype(BF)
    select_ref[...] = select
    for j, at in enumerate(range(0, width, step)):
        cols = pl.ds(at, step)
        for copy in copies[j]:
            copy.wait()
        x = dot(select, tokens_ref[:, cols], 1, 0).astype(BF)
        z = (dot(select, upstream_ref[:, cols], 1, 0) * scale).astype(BF)
        for k in range(window):
            part = slice(k * CAP, (k + 1) * CAP)
            blocks[k][:CAP, cols] = x[part]
            blocks[k][CAP:, cols] = z[part]


def expert_kernel(count, *refs):
    blocks, refs = refs[:count], refs[count:]
    gate_ref, up_ref, down_ref, x_ref, z_ref, dg_ref, du_ref, hidden_ref = refs[:8]
    parts = refs[8:]
    for j, block in enumerate(blocks):
        x_ref[j * CAP : (j + 1) * CAP, :] = block[:CAP, :]
        z_ref[j * CAP : (j + 1) * CAP, :] = block[CAP:, :]
    x = x_ref[...]
    pre_gate = dot(x, gate_ref[...], 1, 1)
    pre_up = dot(x, up_ref[...], 1, 1)
    d_hidden = dot(z_ref[...], down_ref[...], 1, 1)
    sigma = 1.0 / (1.0 + jnp.exp(-pre_gate))
    active = pre_gate * sigma
    hidden_ref[...] = (active * pre_up).astype(BF)
    d_gate = (d_hidden * pre_up * sigma * (1.0 + pre_gate * (1.0 - sigma))).astype(BF)
    d_up = (d_hidden * active).astype(BF)
    dg_ref[...] = d_gate
    du_ref[...] = d_up
    half = count * CAP // 2
    width = gate_ref.shape[1]
    step = min(STEP, width)
    for at in range(0, width, step):
        cols = pl.ds(at, step)
        value = dot(d_gate, gate_ref[:, cols], 1, 0) + dot(d_up, up_ref[:, cols], 1, 0)
        value = value.astype(BF)
        parts[0][:, cols] = value[:half]
        parts[1][:, cols] = value[half:]


def grad_kernel(count, *refs):
    lefts, rights, outs = refs[: 3 * count], refs[3 * count : 5 * count], refs[5 * count :]
    for m, out in enumerate(outs):
        total = None
        for j in range(count):
            right = rights[j + (count if m == 2 else 0)]
            term = dot(lefts[m * count + j][...], right[...], 0, 0)
            total = term if total is None else total + term
        out[...] = total.astype(BF)


def sum_kernel(terms, *refs):
    outs = refs[terms:]
    rows = outs[0].shape[0]
    for j, out in enumerate(outs):
        total = refs[0][j * rows : (j + 1) * rows, :].astype(F32)
        for ref in refs[1:terms]:
            total = total + ref[j * rows : (j + 1) * rows, :].astype(F32)
        out[...] = total.astype(BF)


def unpack_kernel(count, select_ref, *refs):
    out = refs[-1]
    width = out.shape[1]
    step = min(STEP, width)
    for at in range(0, width, step):
        cols = pl.ds(at, step)
        rows = jnp.concatenate([refs[k][:, cols] for k in range(count)], axis=0)
        out[:, cols] = dot(select_ref[...], rows, 0, 0).astype(BF)


def call(kernel, out_shape, *args, mib=24):
    return pl.pallas_call(
        kernel,
        out_shape=out_shape,
        in_specs=[VMEM] * len(args),
        out_specs=jax.tree.map(lambda _: VMEM, out_shape),
        compiler_params=params(mib),
    )(*args)


def shape(*dims):
    return jax.ShapeDtypeStruct(dims, BF)


def whole(a):
    return pl.BlockSpec(a.shape, lambda i: (0, 0))


def columns(rows, step):
    return pl.BlockSpec((rows, step), lambda i: (0, i))


def pack(window, own, expert_ids, gate_values, tokens, upstream):
    count, width = tokens.shape
    outs = [shape(window * CAP, count), *[shape(2 * CAP, width)] * window]
    return pl.pallas_call(
        functools.partial(pack_kernel, window),
        out_shape=outs,
        in_specs=[SMEM] + [HBM] * 4,
        out_specs=[VMEM] * len(outs),
        scratch_shapes=[
            pltpu.VMEM(expert_ids.shape, jnp.int32),
            pltpu.VMEM(gate_values.shape, F32),
            pltpu.VMEM(tokens.shape, BF),
            pltpu.VMEM(upstream.shape, BF),
            pltpu.SemaphoreType.DMA((2,)),
            pltpu.SemaphoreType.DMA((2 * (width // min(STEP, width)),)),
        ],
        compiler_params=params(56),
    )(own, expert_ids, gate_values, tokens, upstream)


def fetch_kernel(*refs):
    count = len(refs) // 2
    for source, out in zip(refs[:count], refs[count:]):
        out[...] = source[...]


def grads(lefts, rights):
    count = len(rights) // 2
    hidden, width = lefts[0].shape[1], rights[0].shape[1]
    step = min(STEP, width)
    return pl.pallas_call(
        functools.partial(grad_kernel, count),
        grid=(width // step,),
        out_shape=[shape(hidden, width)] * 3,
        in_specs=[whole(a) for a in lefts] + [columns(a.shape[0], step) for a in rights],
        out_specs=[columns(hidden, step)] * 3,
        compiler_params=params(24),
    )(*lefts, *rights)


def on_device(tokens, upstream, expert_ids, gate_values, w_gate, w_up, w_down):
    devices = lax.axis_size("exp")
    window = devices // TILES
    width = tokens.shape[1]
    hidden = w_gate.shape[1]
    gate, up, down = [
        call(fetch_kernel, shape(*w.shape[1:]), w[0], mib=8) for w in (w_gate, w_up, w_down)
    ]
    own = (lax.axis_index("exp") // TILES).astype(jnp.int32)[None]

    def swap(a, bits):
        return lax.ppermute(a, "exp", [(i, i ^ bits) for i in range(devices)])

    def turn(a, k):
        return lax.ppermute(a, "exp", [(i, (i + k * TILES) % devices) for i in range(devices)])

    def near(block):
        return [block] + [swap(block, bits) for bits in (2, 4, 6)]

    def both(blocks):
        return blocks + [swap(b, 1) for b in blocks]

    def later(values, *first):
        count = len(values)
        return lax.optimization_barrier((*values, *first))[:count]

    def expert(blocks):
        rows = len(blocks) * CAP
        return call(
            functools.partial(expert_kernel, len(blocks)),
            [shape(rows, width)] * 2 + [shape(rows, hidden)] * 3 + [shape(rows // 2, width)] * 2,
            *blocks, gate, up, down,
        )

    select, *packed = pack(window, own, expert_ids.T, gate_values.T, tokens, upstream)
    crossed = [turn(packed[k], k) for k in range(1, window)]
    mine = packed[0]
    across, along = swap(mine, 2), swap(mine, 4)
    *crossed, across, along, gate, up, down = later([*crossed, across, along, gate, up, down])

    def halve(result):
        kept, other = result[5:]
        return call(functools.partial(sum_kernel, 2), [shape(CAP, width)] * 4, kept, swap(other, 1))

    def gather(pieces):
        pieces = [pieces[0]] + [swap(pieces[j], 2 * j) for j in (1, 2, 3)]
        return call(functools.partial(sum_kernel, 4), [shape(CAP, width)], *pieces)[0]

    results, returned = [], []
    for k in range(1, window):
        blocks = near(crossed[k - 1])
        if k == window - 1:
            (along,) = later([along], *blocks)
        results.append(expert(both(blocks)))
        pieces = halve(results[-1])
        returned.append(turn(gather(pieces), window - k))
    (corner,) = later([swap(along, 2)], results[-1][5])
    own_blocks = later(both([mine, across, along, corner]), *pieces)
    results.append(expert(own_blocks))
    returned.append(gather(halve(results[-1])))
    results = results[-1:] + results[:-1]
    returned = returned[-1:] + returned[:-1]
    grad_gate, grad_up, grad_down = grads(
        [r[m] for m in (2, 3, 4) for r in results], [r[m] for m in (0, 1) for r in results]
    )
    d_tokens = call(
        functools.partial(unpack_kernel, window), shape(*tokens.shape), select, *returned
    )
    return (d_tokens, grad_gate[None], grad_up[None], grad_down[None])


def solution(mesh):
    rows = P(("grp", "exp"), None)
    tiles = P("exp", None, None)
    grown = P(("grp", "exp"), None, None)
    return jax.shard_map(
        on_device,
        mesh=mesh,
        in_specs=(rows, rows, rows, rows, tiles, tiles, tiles),
        out_specs=(rows, grown, grown, grown),
        check_vma=False,
    )
```

```python
import functools

import jax
import jax.numpy as jnp
from jax import lax
from jax.experimental import pallas as pl
from jax.experimental.pallas import tpu as pltpu
from jax.sharding import PartitionSpec as P

TILES = 8
CAP = 16
BF = jnp.bfloat16
F32 = jnp.float32
VMEM = pl.BlockSpec(memory_space=pltpu.VMEM)
SMEM = pl.BlockSpec(memory_space=pltpu.SMEM)
HBM = pl.BlockSpec(memory_space=pltpu.HBM)
STEP = 1024


def padded(columns):
    return -(-columns // 128) * 128


def params(mib):
    return pltpu.CompilerParams(vmem_limit_bytes=mib * 1024 * 1024)


def dot(left, right, left_dim, right_dim):
    return lax.dot_general(
        left, right, (((left_dim,), (right_dim,)), ((), ())), preferred_element_type=F32
    )


def pack_kernel(window, own_ref, ids_hbm, gate_hbm, tokens_hbm, upstream_hbm, *refs):
    select_ref, blocks = refs[0], refs[1 : window + 1]
    ids_ref, gate_ref, tokens_ref, upstream_ref, small, large = refs[window + 1 :]
    count, width = tokens_ref.shape
    first_copies = [
        pltpu.make_async_copy(ids_hbm, ids_ref, small.at[0]),
        pltpu.make_async_copy(gate_hbm, gate_ref, small.at[1]),
    ]
    step = min(STEP, width)
    copies = []
    for j, at in enumerate(range(0, width, step)):
        cols = pl.ds(at, step)
        copies.append(
            (
                pltpu.make_async_copy(tokens_hbm.at[:, cols], tokens_ref.at[:, cols], large.at[2 * j]),
                pltpu.make_async_copy(
                    upstream_hbm.at[:, cols], upstream_ref.at[:, cols], large.at[2 * j + 1]
                ),
            )
        )
    for copy in first_copies:
        copy.start()
    for pair in copies:
        for copy in pair:
            copy.start()
    for copy in first_copies:
        copy.wait()
    ids = ids_ref[...]
    inside = ids < window
    chosen = jnp.sum(jnp.where(inside, ids, 0).astype(F32), axis=0, keepdims=True).astype(jnp.int32)
    has_slot = jnp.sum(inside.astype(F32), axis=0, keepdims=True) > 0.0
    weight = jnp.sum(jnp.where(inside, gate_ref[...], 0.0), axis=0, keepdims=True)
    shift = chosen - own_ref[0]
    shift = jnp.where(shift < 0, shift + window, shift)
    slots = window * CAP
    slot = lax.broadcasted_iota(jnp.int32, (slots, count), 0)
    first = shift * CAP
    member = ((slot >= first) & (slot < first + CAP) & has_slot).astype(F32)
    row = lax.broadcasted_iota(jnp.int32, (count, count), 0)
    col = lax.broadcasted_iota(jnp.int32, (count, count), 1)
    before = (row < col).astype(BF)
    earlier = dot(member.astype(BF), before, 1, 0)
    select = ((member > 0.0) & ((slot - first).astype(F32) == earlier)).astype(F32)
    scale = jnp.sum(select * weight, axis=1, keepdims=True)
    select = select.astype(BF)
    select_ref[...] = select
    for j, at in enumerate(range(0, width, step)):
        cols = pl.ds(at, step)
        for copy in copies[j]:
            copy.wait()
        x = dot(select, tokens_ref[:, cols], 1, 0).astype(BF)
        z = (dot(select, upstream_ref[:, cols], 1, 0) * scale).astype(BF)
        for k in range(window):
            part = slice(k * CAP, (k + 1) * CAP)
            blocks[k][:CAP, cols] = x[part]
            blocks[k][CAP:, cols] = z[part]


def expert_kernel(count, hidden, *refs):
    blocks, weights = refs[:count], refs[count : count + 2]
    shared_ref, unit_ref, *parts = refs[count + 2 :]
    rows = count * CAP
    for j, block in enumerate(blocks):
        shared_ref[j * CAP : (j + 1) * CAP, :] = block[:CAP, :]
        shared_ref[rows + j * CAP : rows + (j + 1) * CAP, :] = block[CAP:, :]
    x, z = shared_ref[:rows, :], shared_ref[rows : 2 * rows, :]
    terms = []
    for ref, unit_rows, out in ((weights[0], 0, unit_ref), (weights[1], 2 * rows, shared_ref)):
        pre_gate = dot(x, ref[:hidden, :], 1, 1)
        pre_up = dot(x, ref[hidden : 2 * hidden, :], 1, 1)
        d_hidden = dot(z, ref[2 * hidden :, :], 1, 1)
        sigma = 1.0 / (1.0 + jnp.exp(-pre_gate))
        active = pre_gate * sigma
        d_gate = (d_hidden * pre_up * sigma * (1.0 + pre_gate * (1.0 - sigma))).astype(BF)
        d_up = (d_hidden * active).astype(BF)
        for m, unit in enumerate((d_gate, d_up, (active * pre_up).astype(BF))):
            at = m * padded(hidden)
            out[unit_rows : unit_rows + rows, at : at + hidden] = unit
        terms += [(d_gate, ref, 0), (d_up, ref, hidden)]
    width = x.shape[1]
    step = min(STEP, width)
    for at in range(0, width, step):
        cols = pl.ds(at, step)
        value = sum(dot(left, ref[row : row + hidden, cols], 1, 0) for left, ref, row in terms)
        value = value.astype(BF)
        for j, part in enumerate(parts):
            part[:, cols] = value[j * CAP : (j + 1) * CAP]


def grad_kernel(count, *refs):
    units, rows, outs = refs[:count], refs[count : 2 * count], refs[2 * count :]
    hidden, size = outs[0].shape[0], rows[0].shape[0] // 2
    x = jnp.concatenate([r[:size, :] for r in rows], axis=0)
    z = jnp.concatenate([r[size:, :] for r in rows], axis=0)
    for m, (out, right) in enumerate(zip(outs, (x, x, z))):
        at = m * padded(hidden)
        left = jnp.concatenate([u[:, at : at + hidden] for u in units], axis=0)
        out[...] = dot(left, right, 0, 0).astype(BF)


def sum_kernel(terms, *refs):
    outs = refs[terms:]
    rows = outs[0].shape[0]
    for j, out in enumerate(outs):
        total = refs[0][j * rows : (j + 1) * rows, :].astype(F32)
        for ref in refs[1:terms]:
            total = total + ref[j * rows : (j + 1) * rows, :].astype(F32)
        out[...] = total.astype(BF)


def unpack_kernel(count, select_ref, *refs):
    out = refs[-1]
    width = out.shape[1]
    step = min(STEP, width)
    for at in range(0, width, step):
        cols = pl.ds(at, step)
        rows = jnp.concatenate([refs[k][:, cols] for k in range(count)], axis=0)
        out[:, cols] = dot(select_ref[...], rows, 0, 0).astype(BF)


def call(kernel, out_shape, *args, mib=24):
    return pl.pallas_call(
        kernel,
        out_shape=out_shape,
        in_specs=[VMEM] * len(args),
        out_specs=jax.tree.map(lambda _: VMEM, out_shape),
        compiler_params=params(mib),
    )(*args)


def shape(*dims):
    return jax.ShapeDtypeStruct(dims, BF)


def whole(a):
    return pl.BlockSpec(a.shape, lambda i: (0, 0))


def columns(rows, step):
    return pl.BlockSpec((rows, step), lambda i: (0, i))


def pack(window, own, expert_ids, gate_values, tokens, upstream):
    count, width = tokens.shape
    outs = [shape(window * CAP, count), *[shape(2 * CAP, width)] * window]
    return pl.pallas_call(
        functools.partial(pack_kernel, window),
        out_shape=outs,
        in_specs=[SMEM] + [HBM] * 4,
        out_specs=[VMEM] * len(outs),
        scratch_shapes=[
            pltpu.VMEM(expert_ids.shape, jnp.int32),
            pltpu.VMEM(gate_values.shape, F32),
            pltpu.VMEM(tokens.shape, BF),
            pltpu.VMEM(upstream.shape, BF),
            pltpu.SemaphoreType.DMA((2,)),
            pltpu.SemaphoreType.DMA((2 * (width // min(STEP, width)),)),
        ],
        compiler_params=params(56),
    )(own, expert_ids, gate_values, tokens, upstream)


def copy_kernel(source, out):
    out[...] = source[...]


def fetch_kernel(gate_ref, up_ref, down_ref, out_ref):
    rows = gate_ref.shape[0]
    for m, ref in enumerate((gate_ref, up_ref, down_ref)):
        out_ref[m * rows : (m + 1) * rows, :] = ref[...]


def grads(hidden, results):
    count, width = 2 * len(results), results[0][0].shape[1]
    step = min(STEP, width)
    size = results[0][1].shape[0]
    units, unit_specs, rows = [], [], []
    for mine, unit, other in results:
        units += [unit, other]
        unit_specs += [whole(unit), pl.BlockSpec((size, 3 * padded(hidden)), lambda i: (2, 0))]
        rows += [mine, other]
    return pl.pallas_call(
        functools.partial(grad_kernel, count),
        grid=(width // step,),
        out_shape=[shape(hidden, width)] * 3,
        in_specs=unit_specs + [columns(2 * size, step)] * count,
        out_specs=[columns(hidden, step)] * 3,
        compiler_params=params(24),
    )(*units, *rows)


def on_device(tokens, upstream, expert_ids, gate_values, w_gate, w_up, w_down):
    devices = lax.axis_size("exp")
    window = devices // TILES
    width = tokens.shape[1]
    hidden = w_gate.shape[1]
    own = (lax.axis_index("exp") // TILES).astype(jnp.int32)[None]

    def swap(a, bits):
        return lax.ppermute(a, "exp", [(i, i ^ bits) for i in range(devices)])

    def turn(a, k):
        return lax.ppermute(a, "exp", [(i, (i + k * TILES) % devices) for i in range(devices)])

    def near(block):
        return [block] + [swap(block, bits) for bits in (6, 4, 2)]

    def later(values, *first):
        count = len(values)
        return lax.optimization_barrier((*values, *first))[:count]

    def expert(blocks):
        rows = len(blocks) * CAP
        return call(
            functools.partial(expert_kernel, len(blocks), hidden),
            [shape(3 * rows, width), shape(rows, 3 * padded(hidden))] + [shape(CAP, width)] * len(blocks),
            *blocks, weights, sibling,
        )

    select, *packed = pack(window, own, expert_ids.T, gate_values.T, tokens, upstream)
    crossed = [turn(packed[k], k) for k in range(1, window)]
    mine = packed[0]
    along, across = swap(mine, 4), swap(mine, 2)
    weights = call(
        fetch_kernel, shape(3 * hidden, width), *later([w_gate[0], w_up[0], w_down[0]], select)
    )
    crossed = [call(copy_kernel, shape(*c.shape), c, mib=4) for c in crossed]
    *crossed, along, across, weights = later([*crossed, along, across, weights])
    sibling = swap(weights, 1)

    def send(pieces, order=(6, 4, 2)):
        return [pieces[0]] + [swap(piece, bits) for piece, bits in zip(pieces[1:], order)]

    def total(pieces):
        return call(functools.partial(sum_kernel, 4), [shape(CAP, width)], *pieces)[0]

    results, returned = [], []
    for k in range(1, window):
        blocks = near(crossed[k - 1])
        if k == window - 1:
            (along,) = later([along], *blocks)
        shared, unit, *pieces = expert(blocks)
        results.append((shared, unit, swap(shared, 1)))
        sent = send(pieces)
        whole_piece = total(sent)
        returned.append(turn(whole_piece, window - k))
    corner = swap(along, 2)
    own = expert([mine, across, along, corner])
    shared, unit, *own_pieces = later(own, whole_piece)
    results.append((shared, unit, swap(shared, 1)))
    grad_gate, grad_up, grad_down = grads(hidden, results)
    returned = [total(later(send(own_pieces, (2, 4, 6)), grad_gate)), *returned]
    d_tokens = call(
        functools.partial(unpack_kernel, window), shape(*tokens.shape), select, *returned
    )
    return (d_tokens, grad_gate[None], grad_up[None], grad_down[None])


def solution(mesh):
    rows = P(("grp", "exp"), None)
    tiles = P("exp", None, None)
    grown = P(("grp", "exp"), None, None)
    return jax.shard_map(
        on_device,
        mesh=mesh,
        in_specs=(rows, rows, rows, rows, tiles, tiles, tiles),
        out_specs=(rows, grown, grown, grown),
        check_vma=False,
    )
```

```python
import functools

import jax
import jax.numpy as jnp
from jax import lax
from jax.experimental import pallas as pl
from jax.experimental.pallas import tpu as pltpu
from jax.sharding import PartitionSpec as P

TILES = 8
CAP = 16
BF = jnp.bfloat16
F32 = jnp.float32
VMEM = pl.BlockSpec(memory_space=pltpu.VMEM)
SMEM = pl.BlockSpec(memory_space=pltpu.SMEM)
HBM = pl.BlockSpec(memory_space=pltpu.HBM)
STEP = 1024


def padded(columns):
    return -(-columns // 128) * 128


def params(mib):
    return pltpu.CompilerParams(vmem_limit_bytes=mib * 1024 * 1024)


def dot(left, right, left_dim, right_dim):
    return lax.dot_general(
        left, right, (((left_dim,), (right_dim,)), ((), ())), preferred_element_type=F32
    )


def pack_kernel(window, own_ref, ids_hbm, gate_hbm, tokens_hbm, upstream_hbm, *refs):
    select_ref, blocks = refs[0], refs[1 : window + 1]
    ids_ref, gate_ref, tokens_ref, upstream_ref, small, large = refs[window + 1 :]
    count, width = tokens_ref.shape
    first_copies = [
        pltpu.make_async_copy(ids_hbm, ids_ref, small.at[0]),
        pltpu.make_async_copy(gate_hbm, gate_ref, small.at[1]),
    ]
    step = min(2 * STEP, width)
    copies = []
    for j, at in enumerate(range(0, width, step)):
        cols = pl.ds(at, step)
        copies.append(
            (
                pltpu.make_async_copy(tokens_hbm.at[:, cols], tokens_ref.at[:, cols], large.at[2 * j]),
                pltpu.make_async_copy(
                    upstream_hbm.at[:, cols], upstream_ref.at[:, cols], large.at[2 * j + 1]
                ),
            )
        )
    for copy in first_copies:
        copy.start()
    for pair in copies:
        for copy in pair:
            copy.start()
    for copy in first_copies:
        copy.wait()
    ids = ids_ref[...]
    inside = ids < window
    chosen = jnp.sum(jnp.where(inside, ids, 0).astype(F32), axis=0, keepdims=True).astype(jnp.int32)
    has_slot = jnp.sum(inside.astype(F32), axis=0, keepdims=True) > 0.0
    weight = jnp.sum(jnp.where(inside, gate_ref[...], 0.0), axis=0, keepdims=True)
    shift = chosen - own_ref[0]
    shift = jnp.where(shift < 0, shift + window, shift)
    slots = window * CAP
    slot = lax.broadcasted_iota(jnp.int32, (slots, count), 0)
    first = shift * CAP
    member = ((slot >= first) & (slot < first + CAP) & has_slot).astype(F32)
    row = lax.broadcasted_iota(jnp.int32, (count, count), 0)
    col = lax.broadcasted_iota(jnp.int32, (count, count), 1)
    before = (row < col).astype(BF)
    earlier = dot(member.astype(BF), before, 1, 0)
    select = ((member > 0.0) & ((slot - first).astype(F32) == earlier)).astype(F32)
    scale = jnp.sum(select * weight, axis=1, keepdims=True)
    select = select.astype(BF)
    select_ref[...] = select
    for j, at in enumerate(range(0, width, step)):
        cols = pl.ds(at, step)
        for copy in copies[j]:
            copy.wait()
        x = dot(select, tokens_ref[:, cols], 1, 0).astype(BF)
        z = (dot(select, upstream_ref[:, cols], 1, 0) * scale).astype(BF)
        for k in range(window):
            part = slice(k * CAP, (k + 1) * CAP)
            blocks[k][:CAP, cols] = x[part]
            blocks[k][CAP:, cols] = z[part]


def expert_kernel(count, hidden, *refs):
    blocks, weights = refs[:count], refs[count : count + 2]
    shared_ref, unit_ref, *parts = refs[count + 2 :]
    rows = count * CAP
    for j, block in enumerate(blocks):
        shared_ref[j * CAP : (j + 1) * CAP, :] = block[:CAP, :]
        shared_ref[rows + j * CAP : rows + (j + 1) * CAP, :] = block[CAP:, :]
    x, z = shared_ref[:rows, :], shared_ref[rows : 2 * rows, :]
    terms = []
    for ref, unit_rows, out in ((weights[0], 0, unit_ref), (weights[1], 2 * rows, shared_ref)):
        pre_gate = dot(x, ref[:hidden, :], 1, 1)
        pre_up = dot(x, ref[hidden : 2 * hidden, :], 1, 1)
        d_hidden = dot(z, ref[2 * hidden :, :], 1, 1)
        sigma = 1.0 / (1.0 + jnp.exp(-pre_gate))
        active = pre_gate * sigma
        d_gate = (d_hidden * pre_up * sigma * (1.0 + pre_gate * (1.0 - sigma))).astype(BF)
        d_up = (d_hidden * active).astype(BF)
        for m, unit in enumerate((d_gate, d_up, (active * pre_up).astype(BF))):
            at = m * padded(hidden)
            out[unit_rows : unit_rows + rows, at : at + hidden] = unit
        terms += [(d_gate, ref, 0), (d_up, ref, hidden)]
    width = x.shape[1]
    step = min(STEP, width)
    for at in range(0, width, step):
        cols = pl.ds(at, step)
        value = sum(dot(left, ref[row : row + hidden, cols], 1, 0) for left, ref, row in terms)
        value = value.astype(BF)
        for j, part in enumerate(parts):
            part[:, cols] = value[j * CAP : (j + 1) * CAP]


def grad_kernel(count, *refs):
    units, rows, outs = refs[:count], refs[count : 2 * count], refs[2 * count :]
    hidden, size = outs[0].shape[0], rows[0].shape[0] // 2
    x = jnp.concatenate([r[:size, :] for r in rows], axis=0)
    z = jnp.concatenate([r[size:, :] for r in rows], axis=0)
    for m, (out, right) in enumerate(zip(outs, (x, x, z))):
        at = m * padded(hidden)
        left = jnp.concatenate([u[:, at : at + hidden] for u in units], axis=0)
        out[...] = dot(left, right, 0, 0).astype(BF)


def sum_kernel(terms, *refs):
    outs = refs[terms:]
    rows = outs[0].shape[0]
    for j, out in enumerate(outs):
        total = refs[0][j * rows : (j + 1) * rows, :].astype(F32)
        for ref in refs[1:terms]:
            total = total + ref[j * rows : (j + 1) * rows, :].astype(F32)
        out[...] = total.astype(BF)


def unpack_kernel(count, select_ref, *refs):
    rows, (out_hbm, out_ref, done) = refs[:count], refs[count:]
    width = out_ref.shape[1]
    step = min(STEP // 2, width)
    copies = []
    for j, at in enumerate(range(0, width, step)):
        cols = pl.ds(at, step)
        both = jnp.concatenate([ref[:, cols] for ref in rows], axis=0)
        out_ref[:, cols] = dot(select_ref[...], both, 0, 0).astype(BF)
        copies.append(pltpu.make_async_copy(out_ref.at[:, cols], out_hbm.at[:, cols], done.at[j]))
        copies[-1].start()
    for copy in copies:
        copy.wait()


def call(kernel, out_shape, *args, mib=24):
    return pl.pallas_call(
        kernel,
        out_shape=out_shape,
        in_specs=[VMEM] * len(args),
        out_specs=jax.tree.map(lambda _: VMEM, out_shape),
        compiler_params=params(mib),
    )(*args)


def shape(*dims):
    return jax.ShapeDtypeStruct(dims, BF)


def whole(a):
    return pl.BlockSpec(a.shape, lambda i: (0, 0))


def columns(rows, step):
    return pl.BlockSpec((rows, step), lambda i: (0, i))


def pack(window, own, expert_ids, gate_values, tokens, upstream):
    count, width = tokens.shape
    outs = [shape(window * CAP, count), *[shape(2 * CAP, width)] * window]
    return pl.pallas_call(
        functools.partial(pack_kernel, window),
        out_shape=outs,
        in_specs=[SMEM] + [HBM] * 4,
        out_specs=[VMEM] * len(outs),
        scratch_shapes=[
            pltpu.VMEM(expert_ids.shape, jnp.int32),
            pltpu.VMEM(gate_values.shape, F32),
            pltpu.VMEM(tokens.shape, BF),
            pltpu.VMEM(upstream.shape, BF),
            pltpu.SemaphoreType.DMA((2,)),
            pltpu.SemaphoreType.DMA((2 * (width // min(2 * STEP, width)),)),
        ],
        compiler_params=params(56),
    )(own, expert_ids, gate_values, tokens, upstream)


def copy_kernel(source, out):
    out[...] = source[...]


def fetch_kernel(gate_ref, up_ref, down_ref, out_ref):
    rows = gate_ref.shape[0]
    for m, ref in enumerate((gate_ref, up_ref, down_ref)):
        out_ref[m * rows : (m + 1) * rows, :] = ref[...]


def grads(hidden, results):
    count, width = 2 * len(results), results[0][0].shape[1]
    step = min(STEP, width)
    size = results[0][1].shape[0]
    units, unit_specs, rows = [], [], []
    for mine, unit, other in results:
        units += [unit, other]
        unit_specs += [whole(unit), pl.BlockSpec((size, 3 * padded(hidden)), lambda i: (2, 0))]
        rows += [mine, other]
    return pl.pallas_call(
        functools.partial(grad_kernel, count),
        grid=(width // step,),
        out_shape=[shape(hidden, width)] * 3,
        in_specs=unit_specs + [columns(2 * size, step)] * count,
        out_specs=[columns(hidden, step)] * 3,
        compiler_params=params(24),
    )(*units, *rows)


def unpack(select, pieces):
    count, width = select.shape[1], pieces[0].shape[1]
    return pl.pallas_call(
        functools.partial(unpack_kernel, len(pieces)),
        out_shape=shape(count, width),
        in_specs=[VMEM] * (1 + len(pieces)),
        out_specs=HBM,
        scratch_shapes=[
            pltpu.VMEM((count, width), BF),
            pltpu.SemaphoreType.DMA((width // min(STEP // 2, width),)),
        ],
        compiler_params=params(16),
    )(select, *pieces)


def on_device(tokens, upstream, expert_ids, gate_values, w_gate, w_up, w_down):
    devices = lax.axis_size("exp")
    window = devices // TILES
    width = tokens.shape[1]
    hidden = w_gate.shape[1]
    own = (lax.axis_index("exp") // TILES).astype(jnp.int32)[None]

    def swap(a, bits):
        return lax.ppermute(a, "exp", [(i, i ^ bits) for i in range(devices)])

    def turn(a, k):
        return lax.ppermute(a, "exp", [(i, (i + k * TILES) % devices) for i in range(devices)])

    def near(block):
        return [block] + [swap(block, bits) for bits in (6, 4, 2)]

    def later(values, *first):
        count = len(values)
        return lax.optimization_barrier((*values, *first))[:count]

    def expert(blocks):
        rows = len(blocks) * CAP
        return call(
            functools.partial(expert_kernel, len(blocks), hidden),
            [shape(3 * rows, width), shape(rows, 3 * padded(hidden))] + [shape(CAP, width)] * len(blocks),
            *blocks, weights, sibling,
        )

    select, *packed = pack(window, own, expert_ids.T, gate_values.T, tokens, upstream)
    crossed = [turn(packed[k], k) for k in range(1, window)]
    mine = packed[0]
    along, across = swap(mine, 4), swap(mine, 2)
    weights = call(
        fetch_kernel, shape(3 * hidden, width), *later([w_gate[0], w_up[0], w_down[0]], select)
    )
    crossed = [call(copy_kernel, shape(*c.shape), c, mib=4) for c in crossed]
    *crossed, along, across, weights = later([*crossed, along, across, weights])
    sibling = swap(weights, 1)

    def send(pieces, order=(6, 4, 2)):
        return [pieces[0]] + [swap(piece, bits) for piece, bits in zip(pieces[1:], order)]

    def total(pieces):
        return call(functools.partial(sum_kernel, 4), [shape(CAP, width)], *pieces)[0]

    results, returned = [], []
    for k in range(1, window):
        blocks = near(crossed[k - 1])
        if k == window - 1:
            (along,) = later([along], *blocks)
        shared, unit, *pieces = expert(blocks)
        results.append((shared, unit, swap(shared, 1)))
        sent = send(pieces)
        whole_piece = total(sent)
        returned.append(turn(whole_piece, window - k))
    corner = swap(along, 2)
    own = expert([mine, corner, along, across])
    shared, unit, *own_pieces = later(own, whole_piece)
    results.append((shared, unit, swap(shared, 1)))
    grad_gate, grad_up, grad_down = grads(hidden, results)
    returned = [total(later(send(own_pieces), grad_gate)), *returned]
    d_tokens = unpack(select, returned)
    return (d_tokens, grad_gate[None], grad_up[None], grad_down[None])


def solution(mesh):
    rows = P(("grp", "exp"), None)
    tiles = P("exp", None, None)
    grown = P(("grp", "exp"), None, None)
    return jax.shard_map(
        on_device,
        mesh=mesh,
        in_specs=(rows, rows, rows, rows, tiles, tiles, tiles),
        out_specs=(rows, grown, grown, grown),
        check_vma=False,
    )
```

```python
import functools

import jax
import jax.numpy as jnp
from jax import lax
from jax.experimental import pallas as pl
from jax.experimental.pallas import tpu as pltpu
from jax.sharding import PartitionSpec as P

TILES = 8
CAP = 16
BF = jnp.bfloat16
F32 = jnp.float32
VMEM = pl.BlockSpec(memory_space=pltpu.VMEM)
SMEM = pl.BlockSpec(memory_space=pltpu.SMEM)
HBM = pl.BlockSpec(memory_space=pltpu.HBM)
STEP = 1024


def padded(columns):
    return -(-columns // 128) * 128


def params(mib):
    return pltpu.CompilerParams(vmem_limit_bytes=mib * 1024 * 1024)


def dot(left, right, left_dim, right_dim):
    return lax.dot_general(
        left, right, (((left_dim,), (right_dim,)), ((), ())), preferred_element_type=F32
    )


def pack_kernel(window, own_ref, ids_hbm, gate_hbm, tokens_hbm, upstream_hbm, *refs):
    select_ref, blocks = refs[0], refs[1 : window + 1]
    ids_ref, gate_ref, tokens_ref, upstream_ref, small, large = refs[window + 1 :]
    count, width = tokens_ref.shape
    first_copies = [
        pltpu.make_async_copy(ids_hbm, ids_ref, small.at[0]),
        pltpu.make_async_copy(gate_hbm, gate_ref, small.at[1]),
    ]
    step = min(2 * STEP, width)
    copies = []
    for j, at in enumerate(range(0, width, step)):
        cols = pl.ds(at, step)
        copies.append(
            (
                pltpu.make_async_copy(tokens_hbm.at[:, cols], tokens_ref.at[:, cols], large.at[2 * j]),
                pltpu.make_async_copy(
                    upstream_hbm.at[:, cols], upstream_ref.at[:, cols], large.at[2 * j + 1]
                ),
            )
        )
    for copy in first_copies:
        copy.start()
    for pair in copies:
        for copy in pair:
            copy.start()
    for copy in first_copies:
        copy.wait()
    ids = ids_ref[...]
    inside = ids < window
    chosen = jnp.sum(jnp.where(inside, ids, 0).astype(F32), axis=0, keepdims=True).astype(jnp.int32)
    has_slot = jnp.sum(inside.astype(F32), axis=0, keepdims=True) > 0.0
    weight = jnp.sum(jnp.where(inside, gate_ref[...], 0.0), axis=0, keepdims=True)
    shift = chosen - own_ref[0]
    shift = jnp.where(shift < 0, shift + window, shift)
    slots = window * CAP
    slot = lax.broadcasted_iota(jnp.int32, (slots, count), 0)
    first = shift * CAP
    member = ((slot >= first) & (slot < first + CAP) & has_slot).astype(F32)
    row = lax.broadcasted_iota(jnp.int32, (count, count), 0)
    col = lax.broadcasted_iota(jnp.int32, (count, count), 1)
    before = (row < col).astype(BF)
    earlier = dot(member.astype(BF), before, 1, 0)
    select = ((member > 0.0) & ((slot - first).astype(F32) == earlier)).astype(F32)
    scale = jnp.sum(select * weight, axis=1, keepdims=True)
    select = select.astype(BF)
    select_ref[...] = select
    for j, at in enumerate(range(0, width, step)):
        cols = pl.ds(at, step)
        for copy in copies[j]:
            copy.wait()
        x = dot(select, tokens_ref[:, cols], 1, 0).astype(BF)
        z = (dot(select, upstream_ref[:, cols], 1, 0) * scale).astype(BF)
        for k in range(window):
            part = slice(k * CAP, (k + 1) * CAP)
            blocks[k][:CAP, cols] = x[part]
            blocks[k][CAP:, cols] = z[part]


def expert_kernel(count, hidden, *refs):
    blocks, (turned_ref, mine_ref, other_ref, shared_ref, unit_ref, *parts) = refs[:count], refs[count:]
    rows, both = count * CAP, 2 * hidden
    for j, block in enumerate(blocks):
        shared_ref[j * CAP : (j + 1) * CAP, :] = block[:CAP, :]
        shared_ref[rows + j * CAP : rows + (j + 1) * CAP, :] = block[CAP:, :]
    pre = dot(shared_ref[:rows, :], turned_ref[:, : 2 * both], 1, 0)
    d_hidden = dot(shared_ref[rows : 2 * rows, :], turned_ref[:, 2 * both :], 1, 0)
    pre_gate, pre_up = pre[:, :both], pre[:, both:]
    sigma = 1.0 / (1.0 + jnp.exp(-pre_gate))
    active = pre_gate * sigma
    d_gate = (d_hidden * pre_up * sigma * (1.0 + pre_gate * (1.0 - sigma))).astype(BF)
    d_up = (d_hidden * active).astype(BF)
    units = (d_gate, d_up, (active * pre_up).astype(BF))
    terms = []
    for m, unit in enumerate(units):
        at = m * padded(hidden)
        own, sibling = unit[:, :hidden], unit[:, hidden:]
        unit_ref[:, at : at + hidden] = own
        shared_ref[2 * rows :, at : at + hidden] = sibling
        if m < 2:
            terms += [(own, mine_ref, m * hidden), (sibling, other_ref, m * hidden)]
    width = shared_ref.shape[1]
    step = min(STEP, width)
    for at in range(0, width, step):
        cols = pl.ds(at, step)
        value = sum(dot(left, ref[row : row + hidden, cols], 1, 0) for left, ref, row in terms)
        value = value.astype(BF)
        for j, part in enumerate(parts):
            part[:, cols] = value[j * CAP : (j + 1) * CAP]


def grad_kernel(count, *refs):
    units, rows, outs = refs[:count], refs[count : 2 * count], refs[2 * count :]
    hidden, size = outs[0].shape[0], rows[0].shape[0] // 2
    x = jnp.concatenate([r[:size, :] for r in rows], axis=0)
    z = jnp.concatenate([r[size:, :] for r in rows], axis=0)
    for m, (out, right) in enumerate(zip(outs, (x, x, z))):
        at = m * padded(hidden)
        left = jnp.concatenate([u[:, at : at + hidden] for u in units], axis=0)
        out[...] = dot(left, right, 0, 0).astype(BF)


def sum_kernel(terms, *refs):
    outs = refs[terms:]
    rows = outs[0].shape[0]
    for j, out in enumerate(outs):
        total = refs[0][j * rows : (j + 1) * rows, :].astype(F32)
        for ref in refs[1:terms]:
            total = total + ref[j * rows : (j + 1) * rows, :].astype(F32)
        out[...] = total.astype(BF)


def unpack_kernel(count, select_ref, *refs):
    rows, (out_hbm, out_ref, done) = refs[:count], refs[count:]
    width = out_ref.shape[1]
    step = min(STEP // 2, width)
    copies = []
    for j, at in enumerate(range(0, width, step)):
        cols = pl.ds(at, step)
        both = jnp.concatenate([ref[:, cols] for ref in rows], axis=0)
        out_ref[:, cols] = dot(select_ref[...], both, 0, 0).astype(BF)
        copies.append(pltpu.make_async_copy(out_ref.at[:, cols], out_hbm.at[:, cols], done.at[j]))
        copies[-1].start()
    for copy in copies:
        copy.wait()


def call(kernel, out_shape, *args, mib=24):
    return pl.pallas_call(
        kernel,
        out_shape=out_shape,
        in_specs=[VMEM] * len(args),
        out_specs=jax.tree.map(lambda _: VMEM, out_shape),
        compiler_params=params(mib),
    )(*args)


def shape(*dims):
    return jax.ShapeDtypeStruct(dims, BF)


def whole(a):
    return pl.BlockSpec(a.shape, lambda i: (0, 0))


def columns(rows, step):
    return pl.BlockSpec((rows, step), lambda i: (0, i))


def pack(window, own, expert_ids, gate_values, tokens, upstream):
    count, width = tokens.shape
    outs = [shape(window * CAP, count), *[shape(2 * CAP, width)] * window]
    return pl.pallas_call(
        functools.partial(pack_kernel, window),
        out_shape=outs,
        in_specs=[SMEM] + [HBM] * 4,
        out_specs=[VMEM] * len(outs),
        scratch_shapes=[
            pltpu.VMEM(expert_ids.shape, jnp.int32),
            pltpu.VMEM(gate_values.shape, F32),
            pltpu.VMEM(tokens.shape, BF),
            pltpu.VMEM(upstream.shape, BF),
            pltpu.SemaphoreType.DMA((2,)),
            pltpu.SemaphoreType.DMA((2 * (width // min(2 * STEP, width)),)),
        ],
        compiler_params=params(56),
    )(own, expert_ids, gate_values, tokens, upstream)


def copy_kernel(source, out):
    out[...] = source[...]


def turn_kernel(mine_ref, other_ref, out_ref):
    hidden, width = mine_ref.shape[0] // 3, mine_ref.shape[1]
    step = min(STEP // 2, width)
    for m in range(3):
        part = slice(m * hidden, (m + 1) * hidden)
        for at in range(0, width, step):
            cols = pl.ds(at, step)
            rows = jnp.concatenate([mine_ref[part, cols], other_ref[part, cols]], axis=0)
            out_ref[at : at + step, 2 * m * hidden : 2 * (m + 1) * hidden] = rows.T


def fetch_kernel(gate_ref, up_ref, down_ref, out_ref):
    rows = gate_ref.shape[0]
    for m, ref in enumerate((gate_ref, up_ref, down_ref)):
        out_ref[m * rows : (m + 1) * rows, :] = ref[...]


def grads(hidden, results):
    count, width = 2 * len(results), results[0][0].shape[1]
    step = min(STEP, width)
    size = results[0][1].shape[0]
    units, unit_specs, rows = [], [], []
    for mine, unit, other in results:
        units += [unit, other]
        unit_specs += [whole(unit), pl.BlockSpec((size, 3 * padded(hidden)), lambda i: (2, 0))]
        rows += [mine, other]
    return pl.pallas_call(
        functools.partial(grad_kernel, count),
        grid=(width // step,),
        out_shape=[shape(hidden, width)] * 3,
        in_specs=unit_specs + [columns(2 * size, step)] * count,
        out_specs=[columns(hidden, step)] * 3,
        compiler_params=params(24),
    )(*units, *rows)


def unpack(select, pieces):
    count, width = select.shape[1], pieces[0].shape[1]
    return pl.pallas_call(
        functools.partial(unpack_kernel, len(pieces)),
        out_shape=shape(count, width),
        in_specs=[VMEM] * (1 + len(pieces)),
        out_specs=HBM,
        scratch_shapes=[
            pltpu.VMEM((count, width), BF),
            pltpu.SemaphoreType.DMA((width // min(STEP // 2, width),)),
        ],
        compiler_params=params(16),
    )(select, *pieces)


def on_device(tokens, upstream, expert_ids, gate_values, w_gate, w_up, w_down):
    devices = lax.axis_size("exp")
    window = devices // TILES
    width = tokens.shape[1]
    hidden = w_gate.shape[1]
    own = (lax.axis_index("exp") // TILES).astype(jnp.int32)[None]

    def swap(a, bits):
        return lax.ppermute(a, "exp", [(i, i ^ bits) for i in range(devices)])

    def turn(a, k):
        return lax.ppermute(a, "exp", [(i, (i + k * TILES) % devices) for i in range(devices)])

    def near(block):
        return [block] + [swap(block, bits) for bits in (4, 2, 6)]

    def later(values, *first):
        count = len(values)
        return lax.optimization_barrier((*values, *first))[:count]

    def expert(blocks):
        rows = len(blocks) * CAP
        return call(
            functools.partial(expert_kernel, len(blocks), hidden),
            [shape(3 * rows, width), shape(rows, 3 * padded(hidden))] + [shape(CAP, width)] * len(blocks),
            *blocks, turned, weights, sibling,
        )

    select, *packed = pack(window, own, expert_ids.T, gate_values.T, tokens, upstream)
    crossed = [turn(packed[k], k) for k in range(1, window)]
    mine = packed[0]
    along, across = swap(mine, 4), swap(mine, 2)
    weights = call(
        fetch_kernel, shape(3 * hidden, width), *later([w_gate[0], w_up[0], w_down[0]], select)
    )
    crossed = [call(copy_kernel, shape(*c.shape), c, mib=4) for c in crossed]
    *crossed, along, across, weights = later([*crossed, along, across, weights])
    sibling = swap(weights, 1)
    turned = call(turn_kernel, shape(width, 6 * hidden), weights, sibling)

    def send(pieces, order=(4, 2, 6)):
        return [pieces[0]] + [swap(piece, bits) for piece, bits in zip(pieces[1:], order)]

    def total(pieces):
        return call(functools.partial(sum_kernel, 4), [shape(CAP, width)], *pieces)[0]

    results, sent, returned = [], [], []
    for k in range(1, window):
        blocks = near(crossed[k - 1])
        if k == window - 1:
            (along,) = later([along], *blocks, turned)
        shared, unit, *pieces = expert(blocks)
        results.append((shared, unit, swap(shared, 1)))
        sent.append(send(pieces))
    corner = swap(along, 2)
    own = expert([mine, along, corner, across])
    for k in range(1, window):
        whole_piece = total(later(sent[k - 1], own[1]))
        returned.append(turn(whole_piece, window - k))
    shared, unit, *own_pieces = later(own, whole_piece)
    results.append((shared, unit, swap(shared, 1)))
    grad_gate, grad_up, grad_down = grads(hidden, results)
    returned = [total(later(send(own_pieces, (4, 6, 2)), grad_gate)), *returned]
    d_tokens = unpack(select, returned)
    return (d_tokens, grad_gate[None], grad_up[None], grad_down[None])


def solution(mesh):
    rows = P(("grp", "exp"), None)
    tiles = P("exp", None, None)
    grown = P(("grp", "exp"), None, None)
    return jax.shard_map(
        on_device,
        mesh=mesh,
        in_specs=(rows, rows, rows, rows, tiles, tiles, tiles),
        out_specs=(rows, grown, grown, grown),
        check_vma=False,
    )
```

```python
import functools

import jax
import jax.numpy as jnp
from jax import lax
from jax.experimental import pallas as pl
from jax.experimental.pallas import tpu as pltpu
from jax.sharding import PartitionSpec as P

TILES = 8
CAP = 16
BF = jnp.bfloat16
F32 = jnp.float32
VMEM = pl.BlockSpec(memory_space=pltpu.VMEM)
SMEM = pl.BlockSpec(memory_space=pltpu.SMEM)
HBM = pl.BlockSpec(memory_space=pltpu.HBM)
STEP = 1024


def padded(columns):
    return -(-columns // 128) * 128


def params(mib):
    return pltpu.CompilerParams(vmem_limit_bytes=mib * 1024 * 1024)


def dot(left, right, left_dim, right_dim):
    return lax.dot_general(
        left, right, (((left_dim,), (right_dim,)), ((), ())), preferred_element_type=F32
    )


def pack_kernel(window, own_ref, ids_hbm, gate_hbm, tokens_hbm, upstream_hbm, *refs):
    select_ref, blocks = refs[0], refs[1 : window + 1]
    ids_ref, gate_ref, tokens_ref, upstream_ref, small, large = refs[window + 1 :]
    count, width = tokens_ref.shape
    first_copies = [
        pltpu.make_async_copy(ids_hbm, ids_ref, small.at[0]),
        pltpu.make_async_copy(gate_hbm, gate_ref, small.at[1]),
    ]
    step = min(2 * STEP, width)
    copies = []
    for j, at in enumerate(range(0, width, step)):
        cols = pl.ds(at, step)
        copies.append(
            (
                pltpu.make_async_copy(tokens_hbm.at[:, cols], tokens_ref.at[:, cols], large.at[2 * j]),
                pltpu.make_async_copy(
                    upstream_hbm.at[:, cols], upstream_ref.at[:, cols], large.at[2 * j + 1]
                ),
            )
        )
    for copy in first_copies:
        copy.start()
    for pair in copies:
        for copy in pair:
            copy.start()
    for copy in first_copies:
        copy.wait()
    ids = ids_ref[...]
    inside = ids < window
    chosen = jnp.sum(jnp.where(inside, ids, 0).astype(F32), axis=0, keepdims=True).astype(jnp.int32)
    has_slot = jnp.sum(inside.astype(F32), axis=0, keepdims=True) > 0.0
    weight = jnp.sum(jnp.where(inside, gate_ref[...], 0.0), axis=0, keepdims=True)
    shift = chosen - own_ref[0]
    shift = jnp.where(shift < 0, shift + window, shift)
    slots = window * CAP
    slot = lax.broadcasted_iota(jnp.int32, (slots, count), 0)
    first = shift * CAP
    member = ((slot >= first) & (slot < first + CAP) & has_slot).astype(F32)
    row = lax.broadcasted_iota(jnp.int32, (count, count), 0)
    col = lax.broadcasted_iota(jnp.int32, (count, count), 1)
    before = (row < col).astype(BF)
    earlier = dot(member.astype(BF), before, 1, 0)
    select = ((member > 0.0) & ((slot - first).astype(F32) == earlier)).astype(F32)
    scale = jnp.sum(select * weight, axis=1, keepdims=True)
    select = select.astype(BF)
    select_ref[...] = select
    for j, at in enumerate(range(0, width, step)):
        cols = pl.ds(at, step)
        for copy in copies[j]:
            copy.wait()
        x = dot(select, tokens_ref[:, cols], 1, 0).astype(BF)
        z = (dot(select, upstream_ref[:, cols], 1, 0) * scale).astype(BF)
        for k in range(window):
            part = slice(k * CAP, (k + 1) * CAP)
            blocks[k][:CAP, cols] = x[part]
            blocks[k][CAP:, cols] = z[part]


def expert_kernel(count, hidden, *refs):
    blocks, (turned_ref, mine_ref, other_ref, shared_ref, unit_ref, *parts) = refs[:count], refs[count:]
    rows, both = count * CAP, 2 * hidden
    for j, block in enumerate(blocks):
        shared_ref[j * CAP : (j + 1) * CAP, :] = block[:CAP, :]
        shared_ref[rows + j * CAP : rows + (j + 1) * CAP, :] = block[CAP:, :]
    pre = dot(shared_ref[:rows, :], turned_ref[:, : 2 * both], 1, 0)
    d_hidden = dot(shared_ref[rows : 2 * rows, :], turned_ref[:, 2 * both :], 1, 0)
    pre_gate, pre_up = pre[:, :both], pre[:, both:]
    sigma = 1.0 / (1.0 + jnp.exp(-pre_gate))
    active = pre_gate * sigma
    d_gate = (d_hidden * pre_up * sigma * (1.0 + pre_gate * (1.0 - sigma))).astype(BF)
    d_up = (d_hidden * active).astype(BF)
    units = (d_gate, d_up, (active * pre_up).astype(BF))
    terms = []
    for m, unit in enumerate(units):
        at = m * padded(hidden)
        own, sibling = unit[:, :hidden], unit[:, hidden:]
        unit_ref[:, at : at + hidden] = own
        shared_ref[2 * rows :, at : at + hidden] = sibling
        if m < 2:
            terms += [(own, mine_ref, m * hidden), (sibling, other_ref, m * hidden)]
    width = shared_ref.shape[1]
    step = min(STEP, width)
    for at in range(0, width, step):
        cols = pl.ds(at, step)
        value = sum(dot(left, ref[row : row + hidden, cols], 1, 0) for left, ref, row in terms)
        value = value.astype(BF)
        for j, part in enumerate(parts):
            part[:, cols] = value[j * CAP : (j + 1) * CAP]


def grad_kernel(count, *refs):
    units, rows, outs = refs[:count], refs[count : 2 * count], refs[2 * count :]
    hidden, size = outs[0].shape[0], rows[0].shape[0] // 2
    x = jnp.concatenate([r[:size, :] for r in rows], axis=0)
    z = jnp.concatenate([r[size:, :] for r in rows], axis=0)
    for m, (out, right) in enumerate(zip(outs, (x, x, z))):
        at = m * padded(hidden)
        left = jnp.concatenate([u[:, at : at + hidden] for u in units], axis=0)
        out[...] = dot(left, right, 0, 0).astype(BF)


def sum_kernel(terms, *refs):
    outs = refs[terms:]
    rows = outs[0].shape[0]
    for j, out in enumerate(outs):
        total = refs[0][j * rows : (j + 1) * rows, :].astype(F32)
        for ref in refs[1:terms]:
            total = total + ref[j * rows : (j + 1) * rows, :].astype(F32)
        out[...] = total.astype(BF)


def unpack_kernel(count, select_ref, *refs):
    rows, (out_hbm, out_ref, done) = refs[:count], refs[count:]
    width = out_ref.shape[1]
    step = min(STEP // 2, width)
    copies = []
    for j, at in enumerate(range(0, width, step)):
        cols = pl.ds(at, step)
        both = jnp.concatenate([ref[:, cols] for ref in rows], axis=0)
        out_ref[:, cols] = dot(select_ref[...], both, 0, 0).astype(BF)
        copies.append(pltpu.make_async_copy(out_ref.at[:, cols], out_hbm.at[:, cols], done.at[j]))
        copies[-1].start()
    for copy in copies:
        copy.wait()


def call(kernel, out_shape, *args, mib=24):
    return pl.pallas_call(
        kernel,
        out_shape=out_shape,
        in_specs=[VMEM] * len(args),
        out_specs=jax.tree.map(lambda _: VMEM, out_shape),
        compiler_params=params(mib),
    )(*args)


def shape(*dims):
    return jax.ShapeDtypeStruct(dims, BF)


def whole(a):
    return pl.BlockSpec(a.shape, lambda i: (0, 0))


def columns(rows, step):
    return pl.BlockSpec((rows, step), lambda i: (0, i))


def pack(window, own, expert_ids, gate_values, tokens, upstream):
    count, width = tokens.shape
    outs = [shape(window * CAP, count), *[shape(2 * CAP, width)] * window]
    return pl.pallas_call(
        functools.partial(pack_kernel, window),
        out_shape=outs,
        in_specs=[SMEM] + [HBM] * 4,
        out_specs=[VMEM] * len(outs),
        scratch_shapes=[
            pltpu.VMEM(expert_ids.shape, jnp.int32),
            pltpu.VMEM(gate_values.shape, F32),
            pltpu.VMEM(tokens.shape, BF),
            pltpu.VMEM(upstream.shape, BF),
            pltpu.SemaphoreType.DMA((2,)),
            pltpu.SemaphoreType.DMA((2 * (width // min(2 * STEP, width)),)),
        ],
        compiler_params=params(56),
    )(own, expert_ids, gate_values, tokens, upstream)


def copy_kernel(source, out):
    out[...] = source[...]


def turn_kernel(*refs):
    mine, other, out_ref = refs[:2], refs[2:4], refs[4]
    hidden, width = mine[1].shape
    step = min(STEP // 2, width)
    for m in range(3):
        part = slice((m % 2) * hidden, (m % 2 + 1) * hidden)
        for at in range(0, width, step):
            cols = pl.ds(at, step)
            rows = jnp.concatenate([pair[m // 2][part, cols] for pair in (mine, other)], axis=0)
            out_ref[at : at + step, 2 * m * hidden : 2 * (m + 1) * hidden] = rows.T


def fetch_kernel(*refs):
    *sources, out_ref = refs
    rows = sources[0].shape[0]
    for m, ref in enumerate(sources):
        out_ref[m * rows : (m + 1) * rows, :] = ref[...]


def grads(hidden, results):
    count, width = 2 * len(results), results[0][0].shape[1]
    step = min(STEP, width)
    size = results[0][1].shape[0]
    units, unit_specs, rows = [], [], []
    for mine, unit, other in results:
        units += [unit, other]
        unit_specs += [whole(unit), pl.BlockSpec((size, 3 * padded(hidden)), lambda i: (2, 0))]
        rows += [mine, other]
    return pl.pallas_call(
        functools.partial(grad_kernel, count),
        grid=(width // step,),
        out_shape=[shape(hidden, width)] * 3,
        in_specs=unit_specs + [columns(2 * size, step)] * count,
        out_specs=[columns(hidden, step)] * 3,
        compiler_params=params(24),
    )(*units, *rows)


def unpack(select, pieces):
    count, width = select.shape[1], pieces[0].shape[1]
    return pl.pallas_call(
        functools.partial(unpack_kernel, len(pieces)),
        out_shape=shape(count, width),
        in_specs=[VMEM] * (1 + len(pieces)),
        out_specs=HBM,
        scratch_shapes=[
            pltpu.VMEM((count, width), BF),
            pltpu.SemaphoreType.DMA((width // min(STEP // 2, width),)),
        ],
        compiler_params=params(16),
    )(select, *pieces)


def on_device(tokens, upstream, expert_ids, gate_values, w_gate, w_up, w_down):
    devices = lax.axis_size("exp")
    window = devices // TILES
    width = tokens.shape[1]
    hidden = w_gate.shape[1]
    own = (lax.axis_index("exp") // TILES).astype(jnp.int32)[None]

    def swap(a, bits):
        return lax.ppermute(a, "exp", [(i, i ^ bits) for i in range(devices)])

    def turn(a, k):
        return lax.ppermute(a, "exp", [(i, (i + k * TILES) % devices) for i in range(devices)])

    def near(block):
        return [block] + [swap(block, bits) for bits in (4, 2, 6)]

    def later(values, *first):
        count = len(values)
        return lax.optimization_barrier((*values, *first))[:count]

    def expert(blocks):
        rows = len(blocks) * CAP
        return call(
            functools.partial(expert_kernel, len(blocks), hidden),
            [shape(3 * rows, width), shape(rows, 3 * padded(hidden))] + [shape(CAP, width)] * len(blocks),
            *blocks, turned, weights[0], sibling[0],
        )

    select, *packed = pack(window, own, expert_ids.T, gate_values.T, tokens, upstream)
    crossed = [turn(packed[k], k) for k in range(1, window)]
    mine = packed[0]
    along, across = swap(mine, 4), swap(mine, 2)
    gate, up, down = later([w_gate[0], w_up[0], w_down[0]], select)
    weights = [
        call(fetch_kernel, shape(2 * hidden, width), gate, up),
        call(fetch_kernel, shape(hidden, width), down),
    ]
    crossed = [call(copy_kernel, shape(*c.shape), c, mib=4) for c in crossed]
    *crossed, along, across, weights[0], weights[1] = later([*crossed, along, across, *weights])
    sibling = [swap(w, 1) for w in weights]
    turned = call(turn_kernel, shape(width, 6 * hidden), *weights, *sibling)

    def send(pieces, order=(4, 2, 6)):
        return [pieces[0]] + [swap(piece, bits) for piece, bits in zip(pieces[1:], order)]

    def total(pieces):
        return call(functools.partial(sum_kernel, 4), [shape(CAP, width)], *pieces)[0]

    results, sent, returned = [], [], []
    for k in range(1, window):
        blocks = near(crossed[k - 1])
        if k == window - 1:
            (along,) = later([along], *blocks, turned)
        shared, unit, *pieces = expert(blocks)
        results.append((shared, unit, swap(shared, 1)))
        sent.append(send(pieces))
    corner = swap(along, 2)
    own = expert([mine, along, corner, across])
    for k in range(1, window):
        whole_piece = total(later(sent[k - 1], own[1]))
        returned.append(turn(whole_piece, window - k))
    shared, unit, *own_pieces = later(own, whole_piece)
    results.append((shared, unit, swap(shared, 1)))
    grad_gate, grad_up, grad_down = grads(hidden, results)
    returned = [total(later(send(own_pieces, (4, 6, 2)), grad_gate)), *returned]
    d_tokens = unpack(select, returned)
    return (d_tokens, grad_gate[None], grad_up[None], grad_down[None])


def solution(mesh):
    rows = P(("grp", "exp"), None)
    tiles = P("exp", None, None)
    grown = P(("grp", "exp"), None, None)
    return jax.shard_map(
        on_device,
        mesh=mesh,
        in_specs=(rows, rows, rows, rows, tiles, tiles, tiles),
        out_specs=(rows, grown, grown, grown),
        check_vma=False,
    )
```
